512 devices in a mesh: row: 32 (over y, x, core), col: 16 (over z).
Axes of the slice: x: 4, y: 4, z: 16, core: 2. Of those that a mesh axis runs over, the one named last changes fastest.
Arguments:
- tokens: float32 [512, 6144], P('row', 'col'), may hold values from -6 to 6
- weight_in: float32 [6144, 12288], P('col', 'row'), may hold values from -0.078125 to 0.078125
- weight_out: float32 [12288, 6144], P('row', 'col'), may hold values from -0.0546875 to 0.0546875
- cotangent: float32 [512, 6144], P('row', 'col'), may hold values from -1.5 to 1.5
Outputs:
- output: float32 [512, 6144], P('row', 'col')
- input_grad: float32 [512, 6144], P('row', 'col')
- weight_in_grad: float32 [6144, 12288], P('col', 'row')
- weight_out_grad: float32 [12288, 6144], P('row', 'col')
The draws below stay inside these ranges and needn't reach their ends.
All inputs are finite; a program needn't handle non-finite values.
Results may differ from the reference program's by a relative error of at most 0.00012.
Values sent between devices are 32-bit elements; how exact they have to be, the bound alone decides.
No kernel may reach another device: no remote copies, remote signals or barrier semaphores. Data moves between devices by JAX's collectives and lax.ppermute only.
A program may use at most 64 MiB of HBM per device.

```python
import math
import jax
import jax.numpy as jnp
from jax import lax

D = 6144
FF = 12288
TOKENS = 512


def steps_of(rng, shape, split, least, largest):
    def one(dim, parts):
        heights = jax.random.uniform(jax.random.fold_in(jax.random.fold_in(rng, 6), dim), (parts,), jnp.float32, least / len(split), largest / len(split))
        return jnp.repeat(jnp.exp(heights), shape[dim] // parts).reshape((-1,) + (1,) * (len(shape) - dim - 1))

    loudness = one(*split[0])
    for cut in split[1:]:
        loudness = loudness * one(*cut)
    return loudness


def bell_draw(stream_key, extent, width, limit, shards=(), held_as=jnp.bfloat16):
    drawn = jax.random.normal(stream_key, extent, jnp.float32) * width
    if len(shards) > 0:
        drawn = steps_of(stream_key, extent, shards, -0.22, 0.18) * drawn
    return jnp.clip(drawn, min=-limit, max=limit).astype(held_as)


def setup_inputs(seed: int = 0) -> dict:
    seeds = jax.random.split(jax.random.key(seed), 5)
    tokens = bell_draw(seeds[0], (TOKENS, D), 1.0, 6.0, ((0, 32), (1, 16)), jnp.float32)
    weight_in = bell_draw(seeds[1], (D, FF), D ** -0.5, 0.078125, ((0, 16), (1, 32)), jnp.float32)
    weight_out = bell_draw(seeds[2], (FF, D), FF ** -0.5, 0.0546875, ((0, 32), (1, 16)), jnp.float32)
    cotangent = bell_draw(seeds[3], (TOKENS, D), 0.25, 1.5, ((0, 32), (1, 16)), jnp.float32)
    return {"tokens": tokens, "weight_in": weight_in, "weight_out": weight_out, "cotangent": cotangent}


def product(left, right):
    return jnp.dot(left, right, precision=lax.Precision.HIGHEST, preferred_element_type=jnp.float32)

def gelu_value(pre):
    return pre * 0.5 * (1.0 + jax.scipy.special.erf(pre / math.sqrt(2.0)))

def gelu_slope(pre):
    cumulative = 0.5 * (1.0 + jax.scipy.special.erf(pre / math.sqrt(2.0)))
    density = jnp.exp(-0.5 * pre * pre) / math.sqrt(2.0 * math.pi)
    return cumulative + pre * density

def reference(tokens, weight_in, weight_out, cotangent):
    pre = product(tokens, weight_in)
    act = gelu_value(pre)
    output = product(act, weight_out)
    weight_out_grad = product(act.T, cotangent)
    act_grad = product(cotangent, weight_out.T)
    pre_grad = act_grad * gelu_slope(pre)
    input_grad = product(pre_grad, weight_in.T)
    weight_in_grad = product(tokens.T, pre_grad)
    return (output, input_grad, weight_in_grad, weight_out_grad)
```

```python
import math

import jax
import jax.numpy as jnp
from jax import lax
from jax.sharding import PartitionSpec as P

BOTH = ("row", "col")
HIGH = lax.Precision.HIGH


def dot(left, right, dims):
    return lax.dot_general(left, right, (dims, ((), ())), precision=HIGH, preferred_element_type=jnp.float32)


def gelu_value(pre):
    return pre * 0.5 * (1.0 + jax.scipy.special.erf(pre / math.sqrt(2.0)))


def gelu_slope(pre):
    cumulative = 0.5 * (1.0 + jax.scipy.special.erf(pre / math.sqrt(2.0)))
    density = jnp.exp(-0.5 * pre * pre) / math.sqrt(2.0 * math.pi)
    return cumulative + pre * density


class Plan:
    def __init__(self, rows, cols):
        self.rows, self.cols = rows, cols
        self.ring = cols // 2
        self.steps = self.ring // 2

    def flat(self, row, col):
        return row * self.cols + col

    def partner(self, core, col):
        return (col + (1 if (col + core) % 2 == 0 else -1)) % self.cols

    def peer(self, step, core, place):
        if (step + core) % 2 == 0:
            return place ^ 1
        return (place + 1) % self.ring if place % 2 else (place - 1) % self.ring

    def received(self, step, core, place):
        peer = self.peer(step, core, place)
        if step == 0:
            return [peer]
        if step == 1:
            return self.received(0, core, peer) + [peer]
        return self.received(step - 1, core, peer)

    def own_order(self, core, col):
        place = col // 2
        order = []
        for step in reversed(range(self.steps)):
            order += self.received(step, core, place)
        return [2 * k + col % 2 for k in order + [place]]

    def order(self, core, col):
        return self.own_order(core, self.partner(core, col)) + self.own_order(core, col)

    def chip_groups(self):
        return [
            [self.flat(2 * k + core, col) for k in self.order(core, col)]
            for col in range(self.cols)
            for core in range(2)
        ]

    def neighbour_perm(self):
        return [
            (self.flat(row, col), self.flat(row, self.partner(row % 2, col)))
            for row in range(self.rows)
            for col in range(self.cols)
        ]

    def ring_groups(self, step):
        groups = []
        for row in range(self.rows):
            core = row % 2
            for col in range(self.cols):
                place = col // 2
                if place % 2 == (step + core) % 2:
                    peer = self.peer(step, core, place)
                    groups.append([self.flat(row, col), self.flat(row, 2 * peer + col % 2)])
        return groups


def solution(mesh):
    rows, cols = mesh.shape["row"], mesh.shape["col"]
    plan = Plan(rows, cols)
    half = cols // 2
    chip_groups = plan.chip_groups()
    neighbour_perm = plan.neighbour_perm()
    core_perm = [(row, row ^ 1) for row in range(rows)]

    def local(tokens, weight_in, weight_out, cotangent):
        n, d = tokens.shape
        h = weight_in.shape[1]
        turn = lax.axis_index("row") + (lax.axis_index("col") >> 1)

        def ring_swap(block, step):
            pair = lax.all_gather(block, BOTH, axis=0, axis_index_groups=plan.ring_groups(step))
            return jnp.where((turn + step) & 1 == 0, pair[1], pair[0])

        weight_in_other = lax.ppermute(weight_in, "row", core_perm)
        weight_out_other = lax.ppermute(weight_out, "row", core_perm)

        both = jnp.concatenate([tokens, cotangent], axis=0)
        sent = jnp.broadcast_to(both[None], (cols, 2 * n, d))
        gathered = lax.all_to_all(sent, BOTH, 0, 0, tiled=True, axis_index_groups=chip_groups)
        token_all = gathered[:, :n].reshape(cols * n, d)
        cotangent_all = gathered[:, n:].reshape(cols * n, d)
        cut = half * n

        w_in = jnp.concatenate([weight_in, weight_in_other], axis=1)
        w_out = jnp.concatenate([weight_out, weight_out_other], axis=0)

        pre_away = lax.ppermute(dot(token_all[:cut], w_in, ((1,), (0,))), BOTH, neighbour_perm)
        grad_away = lax.ppermute(dot(cotangent_all[:cut], w_out, ((1,), (1,))), BOTH, neighbour_perm)
        pre_sum = dot(token_all[cut:], w_in, ((1,), (0,))) + pre_away
        grad_sum = dot(cotangent_all[cut:], w_out, ((1,), (1,))) + grad_away
        sums = jnp.stack([pre_sum, grad_sum]).reshape(2, half, n, 2 * h)

        arrived = None
        at = 0
        for step in reversed(range(1, plan.steps)):
            part = sums[:, at : at + 2]
            at += 2
            arrived = ring_swap(part if arrived is None else part + arrived, step)
        last = sums[:, at : at + 1] + arrived[:, :1]
        mine = sums[:, at + 1 :] + arrived[:, 1:] + ring_swap(last, 0)

        pre, grad = mine[0], mine[1]
        own = jnp.stack([gelu_value(pre), grad * gelu_slope(pre)])
        blocks = [own]
        got = ring_swap(own, 0)
        blocks.insert(0, got)
        block = jnp.concatenate([got, own], axis=1)
        for step in range(1, plan.steps):
            block = ring_swap(block, step)
            blocks.insert(0, block)
        hidden = jnp.concatenate(blocks, axis=1).reshape(2, cut, 2 * h)
        act_here, slope_here = hidden[0], hidden[1]
        act_away = lax.ppermute(act_here, BOTH, neighbour_perm)
        slope_away = lax.ppermute(slope_here, BOTH, neighbour_perm)
        act_all = jnp.concatenate([act_away, act_here], axis=0)
        slope_all = jnp.concatenate([slope_away, slope_here], axis=0)

        out_part = dot(act_all, w_out, ((1,), (0,))).reshape(cols, n, d)
        in_part = dot(slope_all, w_in, ((1,), (1,))).reshape(cols, n, d)

        out_other = dot(act_all[:, h:], cotangent_all, ((0,), (0,)))
        in_other = dot(token_all, slope_all[:, h:], ((0,), (0,)))
        out_other = lax.ppermute(out_other, "row", core_perm)
        in_other = lax.ppermute(in_other, "row", core_perm)
        weight_out_grad = dot(act_all[:, :h], cotangent_all, ((0,), (0,))) + out_other
        weight_in_grad = dot(token_all, slope_all[:, :h], ((0,), (0,))) + in_other

        parts = jnp.concatenate([out_part, in_part], axis=1)
        parts = lax.all_to_all(parts, BOTH, 0, 0, tiled=True, axis_index_groups=chip_groups)
        total = jnp.sum(parts, axis=0)
        return (total[:n], total[n:], weight_in_grad, weight_out_grad)

    placed = (P("row", "col"), P("col", "row"), P("row", "col"), P("row", "col"))
    return jax.shard_map(
        local,
        mesh=mesh,
        in_specs=placed,
        out_specs=(P("row", "col"), P("row", "col"), P("col", "row"), P("row", "col")),
        check_vma=False,
    )
```

```python
import math

import jax
import jax.numpy as jnp
from jax import lax
from jax.experimental import pallas as pl
from jax.experimental.pallas import tpu as pltpu
from jax.sharding import PartitionSpec as P

BOTH = ("row", "col")
HIGH = lax.Precision.HIGH


def dot(left, right, dims):
    return lax.dot_general(left, right, (dims, ((), ())), precision=HIGH, preferred_element_type=jnp.float32)


def gelu_value(pre):
    return pre * 0.5 * (1.0 + jax.scipy.special.erf(pre / math.sqrt(2.0)))


def gelu_slope(pre):
    cumulative = 0.5 * (1.0 + jax.scipy.special.erf(pre / math.sqrt(2.0)))
    density = jnp.exp(-0.5 * pre * pre) / math.sqrt(2.0 * math.pi)
    return cumulative + pre * density


def split(value):
    high = value.astype(jnp.bfloat16)
    return high, (value - high.astype(jnp.float32)).astype(jnp.bfloat16)


def over_tokens(left, right):
    def one(a, b):
        return lax.dot_general(a, b, (((0,), (0,)), ((), ())), preferred_element_type=jnp.float32)

    (lh, ll), (rh, rl) = split(left), split(right)
    return one(lh, rh) + (one(lh, rl) + one(ll, rh))


def join_kernel(w_in, w_in_other, w_out, w_out_other, in_joined, out_joined):
    size = w_in.shape[1]
    in_joined[:, :size] = w_in[...]
    in_joined[:, size:] = w_in_other[...]
    out_joined[:size] = w_out[...]
    out_joined[size:] = w_out_other[...]


def join(w_in, w_in_other, w_out, w_out_other):
    d, h = w_in.shape
    return pl.pallas_call(
        join_kernel,
        out_shape=[jax.ShapeDtypeStruct((d, 2 * h), jnp.float32), jax.ShapeDtypeStruct((2 * h, d), jnp.float32)],
        in_specs=[pl.BlockSpec(memory_space=pltpu.VMEM)] * 4,
        out_specs=[pl.BlockSpec(memory_space=pltpu.VMEM)] * 2,
        compiler_params=pltpu.CompilerParams(vmem_limit_bytes=16 * 2**20),
        cost_estimate=pl.CostEstimate(flops=1000, bytes_accessed=1000, transcendentals=0),
    )(w_in, w_in_other, w_out, w_out_other)


def weight_grads_kernel(act_away, act_here, slope_away, slope_here, tokens, cotangent, *rest):
    cut = act_away.shape[0]
    size = cotangent.shape[1]
    outs = rest[-2:]
    at = pl.ds(0, size) if len(rest) == 4 else pl.ds(act_away.shape[1] - size, size)
    grad = over_tokens(act_away[:, at], cotangent[:cut]) + over_tokens(act_here[:, at], cotangent[cut:])
    outs[0][...] = grad + rest[0][...] if len(rest) == 4 else grad
    grad = over_tokens(tokens[:cut], slope_away[:, at]) + over_tokens(tokens[cut:], slope_here[:, at])
    outs[1][...] = grad + rest[1][...] if len(rest) == 4 else grad


def weight_grads(act_away, act_here, slope_away, slope_here, tokens, cotangent, *other):
    size = cotangent.shape[1]
    args = (act_away, act_here, slope_away, slope_here, tokens, cotangent, *other)
    return pl.pallas_call(
        weight_grads_kernel,
        out_shape=[jax.ShapeDtypeStruct((size, size), jnp.float32)] * 2,
        in_specs=[pl.BlockSpec(memory_space=pltpu.VMEM)] * len(args),
        out_specs=[pl.BlockSpec(memory_space=pltpu.VMEM)] * 2,
        compiler_params=pltpu.CompilerParams(vmem_limit_bytes=24 * 2**20),
        cost_estimate=pl.CostEstimate(flops=1000, bytes_accessed=1000, transcendentals=0),
    )(*args)


class Plan:
    def __init__(self, rows, cols):
        self.rows, self.cols = rows, cols
        self.ring = cols // 2

    def flat(self, row, col):
        return row * self.cols + col

    def members(self, core, parity):
        return [2 * ((core + i) % self.ring) + parity for i in range(self.ring)]

    def chip_groups(self):
        groups = []
        for col in range(self.cols):
            for core in range(2):
                order = self.members(core, 1 - col % 2) + self.members(core, col % 2)
                groups.append([self.flat(2 * k + core, col) for k in order])
        return groups

    def neighbour_perm(self, way):
        return [
            (self.flat(row, col), self.flat(row, (col + (way if row % 2 == 0 else -way)) % self.cols))
            for row in range(self.rows)
            for col in range(self.cols)
        ]

    def ring_groups(self):
        return [
            [self.flat(row, col) for col in self.members(row % 2, parity)]
            for row in range(self.rows)
            for parity in range(2)
        ]

    def pair_groups(self, step):
        groups = []
        for ring in self.ring_groups():
            for i in range(step % 2, self.ring, 2):
                groups.append([ring[i], ring[(i + 1) % self.ring]])
        return groups


def solution(mesh):
    rows, cols = mesh.shape["row"], mesh.shape["col"]
    plan = Plan(rows, cols)
    half = cols // 2
    chip_groups = plan.chip_groups()
    ring_groups = plan.ring_groups()
    one_way, other_way = plan.neighbour_perm(1), plan.neighbour_perm(-1)
    core_perm = [(row, row ^ 1) for row in range(rows)]

    def local(tokens, weight_in, weight_out, cotangent):
        n, d = tokens.shape
        h = weight_in.shape[1]
        core = lax.axis_index("row") & 1
        place = ((lax.axis_index("col") >> 1) - core) & (half - 1)
        odd = place & 1
        pair_at = place >> 1
        turn = 2 * odd - 1
        pairs = half // 2

        def pair_swap(block, step):
            got = lax.all_gather(block, BOTH, axis=0, axis_index_groups=plan.pair_groups(step))
            return jnp.where((odd + step) & 1 == 0, got[1], got[0])

        sent = jnp.broadcast_to(jnp.concatenate([tokens, cotangent], axis=0)[None], (cols, 2 * n, d))
        sent, weight_in, weight_out = lax.optimization_barrier((sent, weight_in, weight_out))
        weight_in_other = lax.ppermute(weight_in, "row", core_perm)
        weight_out_other = lax.ppermute(weight_out, "row", core_perm)
        gathered = lax.all_to_all(sent, BOTH, 0, 0, tiled=True, axis_index_groups=chip_groups)
        w_in, w_out = join(weight_in, weight_in_other, weight_out, weight_out_other)
        gathered, w_in, w_out = lax.optimization_barrier((gathered, w_in, w_out))
        token_all = gathered[:, :n].reshape(cols * n, d)
        cotangent_all = gathered[:, n:].reshape(cols * n, d)
        cut = half * n

        pre_away = lax.ppermute(dot(token_all[:cut], w_in, ((1,), (0,))), BOTH, one_way)
        grad_away = lax.ppermute(dot(cotangent_all[:cut], w_out, ((1,), (1,))), BOTH, other_way)
        pre_sum = dot(token_all[cut:], w_in, ((1,), (0,))) + pre_away
        grad_sum = dot(cotangent_all[cut:], w_out, ((1,), (1,))) + grad_away
        sums = jnp.stack([pre_sum, grad_sum]).reshape(2, pairs, 2 * n, 2 * h)

        def pair_sum(at):
            return lax.dynamic_slice_in_dim(sums, at & (pairs - 1), 1, axis=1)

        arrived = pair_swap(pair_sum(pair_at + 2), 3)
        arrived = pair_swap(pair_sum(pair_at - turn) + arrived, 2)
        arrived = pair_swap(pair_sum(pair_at + turn) + arrived, 1)
        last = (pair_sum(pair_at) + arrived).reshape(2, 2, n, 2 * h)
        theirs = jnp.where(odd == 0, last[:, 1], last[:, 0])
        mine = jnp.where(odd == 0, last[:, 0], last[:, 1]) + pair_swap(theirs, 0)

        pre, grad = mine[0], mine[1]
        own = jnp.stack([gelu_value(pre), grad * gelu_slope(pre)])
        ring = lax.all_gather(own, BOTH, axis=0, axis_index_groups=ring_groups)
        act_here = ring[:, 0].reshape(cut, 2 * h)
        slope_here = ring[:, 1].reshape(cut, 2 * h)
        act_away = lax.ppermute(act_here, BOTH, one_way)
        slope_away = lax.ppermute(slope_here, BOTH, other_way)

        def out_rows(act):
            return dot(act, w_out, ((1,), (0,))).reshape(half, n, d)

        def in_rows(slope):
            return dot(slope, w_in, ((1,), (1,))).reshape(half, n, d)

        here = jnp.concatenate([out_rows(act_here), in_rows(slope_here)], axis=1)
        away = jnp.concatenate([out_rows(act_away), in_rows(slope_away)], axis=1)
        parts = jnp.concatenate([away, here], axis=0)
        parts, act_away, slope_away = lax.optimization_barrier((parts, act_away, slope_away))
        parts = lax.all_to_all(parts, BOTH, 0, 0, tiled=True, axis_index_groups=chip_groups)

        hidden = (act_away, act_here, slope_away, slope_here, token_all, cotangent_all)
        out_other, in_other = weight_grads(*hidden)
        out_other = lax.ppermute(out_other, "row", core_perm)
        in_other = lax.ppermute(in_other, "row", core_perm)
        weight_out_grad, weight_in_grad = weight_grads(*hidden, out_other, in_other)

        total = jnp.sum(parts, axis=0)
        return (total[:n], total[n:], weight_in_grad, weight_out_grad)

    placed = (P("row", "col"), P("col", "row"), P("row", "col"), P("row", "col"))
    return jax.shard_map(
        local,
        mesh=mesh,
        in_specs=placed,
        out_specs=(P("row", "col"), P("row", "col"), P("col", "row"), P("row", "col")),
        check_vma=False,
    )
```

```python
import math

import jax
import jax.numpy as jnp
from jax import lax
from jax.experimental import pallas as pl
from jax.experimental.pallas import tpu as pltpu
from jax.sharding import PartitionSpec as P

BOTH = ("row", "col")
VMEM = pl.BlockSpec(memory_space=pltpu.VMEM)


def gelu_value(pre):
    return pre * 0.5 * (1.0 + jax.scipy.special.erf(pre / math.sqrt(2.0)))


def gelu_slope(pre):
    cumulative = 0.5 * (1.0 + jax.scipy.special.erf(pre / math.sqrt(2.0)))
    density = jnp.exp(-0.5 * pre * pre) / math.sqrt(2.0 * math.pi)
    return cumulative + pre * density


def split(value):
    high = value.astype(jnp.bfloat16)
    return high, (value - high.astype(jnp.float32)).astype(jnp.bfloat16)


def three(left, right, dims):
    def one(a, b):
        return lax.dot_general(a, b, (dims, ((), ())), preferred_element_type=jnp.float32)

    (lh, ll), (rh, rl) = split(left), split(right)
    return one(lh, rh) + (one(lh, rl) + one(ll, rh))


PLAIN, RIGHT_T, LEFT_T = ((1,), (0,)), ((1,), (1,)), ((0,), (0,))


def kernel_call(body, out_shapes, args, far=False):
    out = [pltpu.HBM(shape, jnp.float32) if far else jax.ShapeDtypeStruct(shape, jnp.float32) for shape in out_shapes]
    return pl.pallas_call(
        body,
        out_shape=out,
        in_specs=[VMEM] * len(args),
        out_specs=[VMEM] * len(out),
        compiler_params=pltpu.CompilerParams(vmem_limit_bytes=16 * 2**20),
        cost_estimate=pl.CostEstimate(flops=1000, bytes_accessed=1000, transcendentals=0),
    )(*args)


def token_rows(gathered, first, last, which):
    n, d = gathered.shape[1] // 2, gathered.shape[2]
    return gathered[first:last, which * n : (which + 1) * n, :].reshape((last - first) * n, d)


def sums_kernel(first, gathered, w_in, w_in_other, w_out, w_out_other, *outs):
    chips = gathered.shape[0] // 4
    size = w_in.shape[1]
    at = slice(first * chips, (first + len(outs)) * chips)
    for which, (weights, dims) in enumerate((((w_in, w_in_other), PLAIN), ((w_out, w_out_other), RIGHT_T))):
        rows = token_rows(gathered, at.start, at.stop, which)
        for k in range(2):
            term = three(rows, weights[k][...], dims)
            block = term.shape[0] // len(outs) // 2
            for i, out in enumerate(outs):
                for part in range(2):
                    start = (2 * i + part) * block
                    out[part, which, :, k * size : (k + 1) * size] = term[start : start + block]


def hidden_rows(blocks, which, at):
    return jnp.concatenate([block[part, which, :, at] for block in blocks for part in range(2)], axis=0)


def back_kernel(first, count, gathered, w_in, w_in_other, w_out, w_out_other, *refs):
    blocks, refs = refs[:count], refs[count:]
    before, (rows, *grads) = refs[: len(refs) - 5], refs[len(refs) - 5 :]
    size = w_in.shape[1]
    chips = count * (gathered.shape[0] // 4)
    n = rows.shape[1] // 2
    units = (slice(0, size), slice(size, 2 * size))
    act = [hidden_rows(blocks, 0, at) for at in units]
    slope = [hidden_rows(blocks, 1, at) for at in units]
    begin = first * (gathered.shape[0] // 4)
    out_rows = three(act[0], w_out[...], PLAIN) + three(act[1], w_out_other[...], PLAIN)
    in_rows = three(slope[0], w_in[...], RIGHT_T) + three(slope[1], w_in_other[...], RIGHT_T)
    rows[:chips, :n, :] = out_rows.reshape(chips, n, size)
    rows[:chips, n:, :] = in_rows.reshape(chips, n, size)
    if before:
        rows[chips:] = before[0][...]
    tokens, cotangent = (token_rows(gathered, begin, begin + chips, which) for which in range(2))
    for k in range(2):
        out_grad = three(act[1 - k], cotangent, LEFT_T)
        in_grad = three(tokens, slope[1 - k], LEFT_T)
        grads[2 * k][...] = out_grad + before[1 + 2 * k][...] if before else out_grad
        grads[2 * k + 1][...] = in_grad + before[2 + 2 * k][...] if before else in_grad


def send_kernel(tokens, cotangent, sent):
    n = tokens.shape[0]
    for k in range(sent.shape[0]):
        sent[k, :n] = tokens[...]
        sent[k, n:] = cotangent[...]


def collect_kernel(parts, output, input_grad):
    n = output.shape[0]
    output[...] = jnp.sum(parts[:, :n], axis=0)
    input_grad[...] = jnp.sum(parts[:, n:], axis=0)


class Plan:
    def __init__(self, rows, cols):
        self.rows, self.cols = rows, cols

    def flat(self, row, col):
        return row * self.cols + col

    def steps(self, core, col):
        near = 1 if (col + core) % 2 == 0 else -1
        far = 2 if (col // 2 + core) % 2 == 0 else -2
        return near, -near, far

    def planes(self):
        return [
            [
                self.flat(2 * chip + core, col)
                for step in (*self.steps(core, col), 0)
                for chip in range((col + step) % 4, self.rows // 2, 4)
            ]
            for core in range(2)
            for col in range(self.cols)
        ]

    def swap(self, k):
        return [
            (self.flat(row, col), self.flat(row, (col + self.steps(row % 2, col)[k]) % self.cols))
            for row in range(self.rows)
            for col in range(self.cols)
        ]

    def quarter(self, core, col):
        return (col // 4 - core) % 4

    def pairs(self, mates):
        groups = []
        for row in range(self.rows):
            for col in range(self.cols):
                at = self.quarter(row % 2, col)
                if mates and at % 2 == 0:
                    groups.append([self.flat(row, col), self.flat(row, (col + 4) % self.cols)])
                if not mates and at < 2:
                    step = 4 if at == 1 else -4
                    groups.append([self.flat(row, col), self.flat(row, (col + step) % self.cols)])
        return groups


def solution(mesh):
    rows, cols = mesh.shape["row"], mesh.shape["col"]
    plan = Plan(rows, cols)
    planes = plan.planes()
    swaps = [plan.swap(k) for k in range(3)]
    core_perm = [(row, row ^ 1) for row in range(rows)]
    across, mates = plan.pairs(False), plan.pairs(True)

    def local(tokens, weight_in, weight_out, cotangent):
        n, d = tokens.shape
        h = weight_in.shape[1]
        chips = rows // 2
        block = (2, 2, chips // 8 * n, 2 * h)
        at = ((lax.axis_index("col") >> 2) - (lax.axis_index("row") & 1)) & 3
        keep = at >> 1

        sent = kernel_call(send_kernel, [(chips, 2 * n, d)], (tokens, cotangent))[0]
        sent, weight_in, weight_out = lax.optimization_barrier((sent, weight_in, weight_out))
        weight_in_other = lax.ppermute(weight_in, "row", core_perm)
        weight_out_other = lax.ppermute(weight_out, "row", core_perm)
        gathered = lax.all_to_all(sent, BOTH, 0, 0, tiled=True, axis_index_groups=planes)
        weights = (weight_in, weight_in_other, weight_out, weight_out_other)

        away = kernel_call(lambda *refs: sums_kernel(0, *refs), [block] * 3, (gathered, *weights))
        away = [lax.ppermute(value, BOTH, perm) for value, perm in zip(away, swaps)]
        own = kernel_call(lambda *refs: sums_kernel(3, *refs), [block], (gathered, *weights))[0]
        total = own + away[0] + away[1] + away[2]

        def swap(value, groups, first):
            got = lax.all_gather(value, BOTH, axis=0, axis_index_groups=groups)
            return jnp.where(first == 0, got[1], got[0])

        kept = lax.dynamic_index_in_dim(total, keep, 0, keepdims=False)
        given = lax.dynamic_index_in_dim(total, 1 - keep, 0, keepdims=False)
        kept = kept + swap(given, across, keep)
        kept = kept + swap(kept, mates, at & 1)

        pre, grad = kept[0], kept[1]
        hidden = jnp.stack([gelu_value(pre), grad * gelu_slope(pre)])
        own = lax.all_gather(hidden, BOTH, axis=0, axis_index_groups=across)
        blocks = [lax.ppermute(own, BOTH, perm) for perm in swaps] + [own]

        square = [(d, h)] * 4
        early = kernel_call(
            lambda *refs: back_kernel(2, 2, *refs), [(chips // 2, 2 * n, d)] + square, (gathered, *weights, *blocks[2:])
        )
        parts, *grads = kernel_call(
            lambda *refs: back_kernel(0, 2, *refs),
            [(chips, 2 * n, d)] + square,
            (gathered, *weights, *blocks[:2], *early),
            far=True,
        )
        parts = lax.all_to_all(parts, BOTH, 0, 0, tiled=True, axis_index_groups=planes)
        weight_out_grad = grads[2] + lax.ppermute(grads[0], "row", core_perm)
        weight_in_grad = grads[3] + lax.ppermute(grads[1], "row", core_perm)
        output, input_grad = kernel_call(collect_kernel, [(n, d)] * 2, (parts,))
        return (output, input_grad, weight_in_grad, weight_out_grad)

    placed = (P("row", "col"), P("col", "row"), P("row", "col"), P("row", "col"))
    return jax.shard_map(
        local,
        mesh=mesh,
        in_specs=placed,
        out_specs=(P("row", "col"), P("row", "col"), P("col", "row"), P("row", "col")),
        check_vma=False,
    )
```

```python
import math

import jax
import jax.numpy as jnp
from jax import lax
from jax.experimental import pallas as pl
from jax.experimental.pallas import tpu as pltpu
from jax.sharding import PartitionSpec as P

BOTH = ("row", "col")
VMEM = pl.BlockSpec(memory_space=pltpu.VMEM)
SMEM = pl.BlockSpec(memory_space=pltpu.SMEM)
FAR = pl.BlockSpec(memory_space=pltpu.HBM)


def gelu_value(pre):
    return pre * 0.5 * (1.0 + jax.scipy.special.erf(pre / math.sqrt(2.0)))


def gelu_slope(pre):
    cumulative = 0.5 * (1.0 + jax.scipy.special.erf(pre / math.sqrt(2.0)))
    density = jnp.exp(-0.5 * pre * pre) / math.sqrt(2.0 * math.pi)
    return cumulative + pre * density


def split(value):
    high = value.astype(jnp.bfloat16)
    return high, (value - high.astype(jnp.float32)).astype(jnp.bfloat16)


def three(left, right, dims):
    def one(a, b):
        return lax.dot_general(a, b, (dims, ((), ())), preferred_element_type=jnp.float32)

    (lh, ll), (rh, rl) = left, right
    return one(lh, rh) + (one(lh, rl) + one(ll, rh))


def join_kernel(w_in, w_in_other, w_out, w_out_other, in_parts, out_parts):
    size = w_in.shape[1]
    for k, (v, w) in enumerate(((w_in, w_out), (w_in_other, w_out_other))):
        at = slice(k * size, (k + 1) * size)
        in_parts[0, :, at], in_parts[1, :, at] = split(v[...])
        out_parts[0, at, :], out_parts[1, at, :] = split(w[...])


PLAIN, RIGHT_T, LEFT_T = ((1,), (0,)), ((1,), (1,)), ((0,), (0,))


def kernel_call(body, out_shapes, args, kept_as=jnp.float32):
    out = [jax.ShapeDtypeStruct(shape, kept_as) for shape in out_shapes]
    return pl.pallas_call(
        body,
        out_shape=out,
        in_specs=[VMEM] * len(args),
        out_specs=[VMEM] * len(out),
        compiler_params=pltpu.CompilerParams(vmem_limit_bytes=9 * 2**20),
        cost_estimate=pl.CostEstimate(flops=1000, bytes_accessed=1000, transcendentals=0),
    )(*args)


def token_rows(gathered, first, last, which):
    n, d = gathered.shape[1] // 2, gathered.shape[2]
    return gathered[first:last, which * n : (which + 1) * n, :].reshape((last - first) * n, d)


def sums_kernel(first, gathered, w_in, w_out, *outs):
    chips = gathered.shape[0] // 4
    for which, (weight, dims) in enumerate(((w_in, PLAIN), (w_out, RIGHT_T))):
        rows = split(token_rows(gathered, first * chips, (first + len(outs)) * chips, which))
        term = three(rows, (weight[0], weight[1]), dims)
        block = term.shape[0] // len(outs) // 2
        for i, out in enumerate(outs):
            for part in range(2):
                start = (2 * i + part) * block
                out[part, which] = term[start : start + block]


def halves_kernel(keep, *refs):
    terms, (kept, given) = refs[:-2], refs[-2:]
    for out, half in ((kept, keep[0]), (given, 1 - keep[0])):
        total = terms[0][half]
        for term in terms[1:]:
            total = total + term[half]
        out[...] = total


def hidden_rows(blocks, which):
    return jnp.concatenate([block[part, which] for block in blocks for part in range(2)], axis=0)


def back_terms(first, count, gathered, w_in, w_out, blocks):
    size = gathered.shape[2]
    quarter = gathered.shape[0] // 4
    begin, end = first * quarter, (first + count) * quarter
    act, slope = split(hidden_rows(blocks, 0)), split(hidden_rows(blocks, 1))
    tokens, cotangent = (split(token_rows(gathered, begin, end, which)) for which in range(2))
    for k in range(2):
        at = slice((1 - k) * size, (2 - k) * size)
        yield three([v[:, at] for v in act], cotangent, LEFT_T)
        yield three(tokens, [v[:, at] for v in slope], LEFT_T)
    shape = (count * quarter, gathered.shape[1] // 2, size)
    yield three(act, (w_out[0], w_out[1]), PLAIN).reshape(shape)
    yield three(slope, (w_in[0], w_in[1]), RIGHT_T).reshape(shape)


def early_kernel(gathered, w_in, w_out, *refs):
    rows, *grads = refs[2:]
    n = rows.shape[1] // 2
    for k, term in enumerate(back_terms(2, 2, gathered, w_in, w_out, refs[:2])):
        if k < 4:
            grads[k][...] = term
        else:
            rows[:, (k - 4) * n : (k - 3) * n, :] = term


def late_kernel(gathered, w_in, w_out, *refs):
    blocks, (early_rows, *early), refs = refs[:2], refs[2:7], refs[7:]
    parts, grads, rows, scratch, done = refs[0], refs[1:5], refs[5], refs[6], refs[7]
    n = rows.shape[1] // 2
    chips = rows.shape[0] // 2
    copies = [pltpu.make_async_copy(scratch.at[k], grads[k], done.at[k]) for k in range(4)]
    copies.append(pltpu.make_async_copy(rows, parts, done.at[4]))
    rows[chips:] = early_rows[...]
    for k, term in enumerate(back_terms(0, 2, gathered, w_in, w_out, blocks)):
        if k < 4:
            scratch[k] = term + early[k][...]
            copies[k].start()
        else:
            rows[:chips, (k - 4) * n : (k - 3) * n, :] = term
    copies[4].start()
    for copy in copies:
        copy.wait()


def collect_kernel(parts, output, input_grad):
    n = output.shape[0]
    output[...] = jnp.sum(parts[:, :n], axis=0)
    input_grad[...] = jnp.sum(parts[:, n:], axis=0)


class Plan:
    def __init__(self, rows, cols):
        self.rows, self.cols = rows, cols

    def flat(self, row, col):
        return row * self.cols + col

    def steps(self, core, col):
        near = 1 if (col + core) % 2 == 0 else -1
        far = 2 if (col // 2 + core) % 2 == 0 else -2
        return near, -near, far

    def planes(self):
        return [
            [
                self.flat(2 * chip + core, col)
                for step in (*self.steps(core, col), 0)
                for chip in range((col + step) % 4, self.rows // 2, 4)
            ]
            for core in range(2)
            for col in range(self.cols)
        ]

    def swap(self, k):
        return [
            (self.flat(row, col), self.flat(row, (col + self.steps(row % 2, col)[k]) % self.cols))
            for row in range(self.rows)
            for col in range(self.cols)
        ]

    def quarter(self, core, col):
        return (col // 4 - core) % 4

    def pairs(self, mates):
        groups = []
        for row in range(self.rows):
            for col in range(self.cols):
                at = self.quarter(row % 2, col)
                if mates and at % 2 == 0:
                    groups.append([self.flat(row, col), self.flat(row, (col + 4) % self.cols)])
                if not mates and at < 2:
                    step = 4 if at == 1 else -4
                    groups.append([self.flat(row, col), self.flat(row, (col + step) % self.cols)])
        return groups


def solution(mesh):
    rows, cols = mesh.shape["row"], mesh.shape["col"]
    plan = Plan(rows, cols)
    planes = plan.planes()
    swaps = [plan.swap(k) for k in range(3)]
    core_perm = [(row, row ^ 1) for row in range(rows)]
    across, mates = plan.pairs(False), plan.pairs(True)

    def local(tokens, weight_in, weight_out, cotangent):
        n, d = tokens.shape
        h = weight_in.shape[1]
        chips = rows // 2
        block = (2, 2, chips // 8 * n, 2 * h)
        at = ((lax.axis_index("col") >> 2) - (lax.axis_index("row") & 1)) & 3
        keep = at >> 1

        sent = jnp.broadcast_to(jnp.concatenate([tokens, cotangent], axis=0)[None], (chips, 2 * n, d))
        sent, weight_in, weight_out = lax.optimization_barrier((sent, weight_in, weight_out))
        weight_in_other = lax.ppermute(weight_in, "row", core_perm)
        weight_out_other = lax.ppermute(weight_out, "row", core_perm)
        gathered = lax.all_to_all(sent, BOTH, 0, 0, tiled=True, axis_index_groups=planes)
        weights = kernel_call(
            join_kernel,
            [(2, d, 2 * h), (2, 2 * h, d)],
            (weight_in, weight_in_other, weight_out, weight_out_other),
            kept_as=jnp.bfloat16,
        )
        gathered, *weights = lax.optimization_barrier((gathered, *weights))

        away = kernel_call(lambda *refs: sums_kernel(0, *refs), [block] * 3, (gathered, *weights))
        away = [lax.ppermute(value, BOTH, perm) for value, perm in zip(away, swaps)]
        own = kernel_call(lambda *refs: sums_kernel(3, *refs), [block], (gathered, *weights))[0]
        kept, given = pl.pallas_call(
            halves_kernel,
            out_shape=[jax.ShapeDtypeStruct(block[1:], jnp.float32)] * 2,
            in_specs=[SMEM] + [VMEM] * 4,
            out_specs=[VMEM] * 2,
            compiler_params=pltpu.CompilerParams(vmem_limit_bytes=9 * 2**20),
            cost_estimate=pl.CostEstimate(flops=1000, bytes_accessed=1000, transcendentals=0),
        )(keep.astype(jnp.int32).reshape(1), own, *away)

        def swap(value, groups, first):
            got = lax.all_gather(value, BOTH, axis=0, axis_index_groups=groups)
            return jnp.where(first == 0, got[1], got[0])

        kept = kept + swap(given, across, keep)
        kept = kept + swap(kept, mates, at & 1)

        pre, grad = kept[0], kept[1]
        hidden = jnp.stack([gelu_value(pre), grad * gelu_slope(pre)])
        own = lax.all_gather(hidden, BOTH, axis=0, axis_index_groups=across)
        blocks = [lax.ppermute(own, BOTH, perm) for perm in swaps] + [own]

        square = [(d, h)] * 4
        early = kernel_call(early_kernel, [(chips // 2, 2 * n, d)] + square, (gathered, *weights, *blocks[2:]))
        parts, *grads = pl.pallas_call(
            late_kernel,
            out_shape=[pltpu.HBM(shape, jnp.float32) for shape in [(chips, 2 * n, d)] + square],
            in_specs=[VMEM] * 10,
            out_specs=[FAR] * 5,
            scratch_shapes=[
                pltpu.VMEM((chips, 2 * n, d), jnp.float32),
                pltpu.VMEM((4, d, h), jnp.float32),
                pltpu.SemaphoreType.DMA((5,)),
            ],
            compiler_params=pltpu.CompilerParams(vmem_limit_bytes=9 * 2**20),
            cost_estimate=pl.CostEstimate(flops=1000, bytes_accessed=1000, transcendentals=0),
        )(gathered, *weights, *blocks[:2], *early)
        parts = lax.all_to_all(parts, BOTH, 0, 0, tiled=True, axis_index_groups=planes)
        weight_out_grad = grads[2] + lax.ppermute(grads[0], "row", core_perm)
        weight_in_grad = grads[3] + lax.ppermute(grads[1], "row", core_perm)
        output, input_grad = kernel_call(collect_kernel, [(n, d)] * 2, (parts,))
        return (output, input_grad, weight_in_grad, weight_out_grad)

    placed = (P("row", "col"), P("col", "row"), P("row", "col"), P("row", "col"))
    return jax.shard_map(
        local,
        mesh=mesh,
        in_specs=placed,
        out_specs=(P("row", "col"), P("row", "col"), P("col", "row"), P("row", "col")),
        check_vma=False,
    )
```

```python
import math

import jax
import jax.numpy as jnp
from jax import lax
from jax.experimental import pallas as pl
from jax.experimental.pallas import tpu as pltpu
from jax.sharding import PartitionSpec as P

BOTH = ("row", "col")
VMEM = pl.BlockSpec(memory_space=pltpu.VMEM)
SMEM = pl.BlockSpec(memory_space=pltpu.SMEM)
FAR = pl.BlockSpec(memory_space=pltpu.HBM)


def gelu_value(pre):
    return pre * 0.5 * (1.0 + jax.scipy.special.erf(pre / math.sqrt(2.0)))


def gelu_slope(pre):
    cumulative = 0.5 * (1.0 + jax.scipy.special.erf(pre / math.sqrt(2.0)))
    density = jnp.exp(-0.5 * pre * pre) / math.sqrt(2.0 * math.pi)
    return cumulative + pre * density


def split(value):
    high = value.astype(jnp.bfloat16)
    return high, (value - high.astype(jnp.float32)).astype(jnp.bfloat16)


def three(left, right, dims):
    def one(a, b):
        return lax.dot_general(a, b, (dims, ((), ())), preferred_element_type=jnp.float32)

    (lh, ll), (rh, rl) = left, right
    return one(lh, rh) + (one(lh, rl) + one(ll, rh))


PLAIN, RIGHT_T, LEFT_T = ((1,), (0,)), ((1,), (1,)), ((0,), (0,))


def kernel_call(body, out_shapes, args, scalars=0, far=False):
    out = [pltpu.HBM(shape, jnp.float32) if far else jax.ShapeDtypeStruct(shape, jnp.float32) for shape in out_shapes]
    return pl.pallas_call(
        body,
        out_shape=out,
        in_specs=[SMEM] * scalars + [VMEM] * (len(args) - scalars),
        out_specs=[VMEM] * len(out),
        compiler_params=pltpu.CompilerParams(vmem_limit_bytes=9 * 2**20),
        cost_estimate=pl.CostEstimate(flops=1000, bytes_accessed=1000, transcendentals=0),
    )(*args)


def token_rows(gathered, first, last, which):
    n, d = gathered.shape[1] // 2, gathered.shape[2]
    return gathered[first:last, which * n : (which + 1) * n, :].reshape((last - first) * n, d)


def sums_kernel(first, keeps, gathered, w_in, w_in_other, w_out, w_out_other, *outs):
    count = len(outs) // 2
    n, d = gathered.shape[1] // 2, gathered.shape[2]
    half = gathered.shape[0] // 8
    for which, (weights, dims) in enumerate((((w_in, w_in_other), PLAIN), ((w_out, w_out_other), RIGHT_T))):
        rows = []
        for i in range(first, first + count):
            for part in (1 - keeps[i], keeps[i]):
                chips = pl.ds((2 * i + part) * half, half)
                rows.append(gathered[chips, which * n : (which + 1) * n, :].reshape(half * n, d))
        rows = split(jnp.concatenate(rows, axis=0))
        for k in range(2):
            term = three(rows, split(weights[k][...]), dims)
            for i, out in enumerate(outs):
                out[which, :, k * d : (k + 1) * d] = term[i * half * n : (i + 1) * half * n]


def add_kernel(*refs):
    total = refs[0][...]
    for ref in refs[1:-1]:
        total = total + ref[...]
    refs[-1][...] = total


def hidden_rows(blocks, which):
    return jnp.concatenate([block[part, which] for block in blocks for part in range(2)], axis=0)


def back_terms(first, count, gathered, weights, blocks):
    size = gathered.shape[2]
    quarter = gathered.shape[0] // 4
    begin, end = first * quarter, (first + count) * quarter
    act, slope = split(hidden_rows(blocks, 0)), split(hidden_rows(blocks, 1))
    tokens, cotangent = (split(token_rows(gathered, begin, end, which)) for which in range(2))
    for k in range(2):
        at = slice((1 - k) * size, (2 - k) * size)
        yield three([v[:, at] for v in act], cotangent, LEFT_T)
        yield three(tokens, [v[:, at] for v in slope], LEFT_T)
    shape = (count * quarter, gathered.shape[1] // 2, size)
    w_in, w_in_other, w_out, w_out_other = weights
    for hidden, pair, dims in ((act, (w_out, w_out_other), PLAIN), (slope, (w_in, w_in_other), RIGHT_T)):
        term = [
            three([v[:, k * size : (k + 1) * size] for v in hidden], split(pair[k][...]), dims) for k in range(2)
        ]
        yield (term[0] + term[1]).reshape(shape)


def early_kernel(gathered, *refs):
    weights, blocks, (rows, *grads) = refs[:4], refs[4:6], refs[6:]
    n = rows.shape[1] // 2
    for k, term in enumerate(back_terms(2, 2, gathered, weights, blocks)):
        if k < 4:
            grads[k][...] = term
        else:
            rows[:, (k - 4) * n : (k - 3) * n, :] = term


def late_kernel(gathered, *refs):
    weights, blocks, (early_rows, *early), refs = refs[:4], refs[4:6], refs[6:11], refs[11:]
    parts, grads, rows, scratch, done = refs[0], refs[1:5], refs[5], refs[6], refs[7]
    n = rows.shape[1] // 2
    chips = rows.shape[0] // 2
    copies = [pltpu.make_async_copy(scratch.at[k], grads[k], done.at[k]) for k in range(4)]
    copies.append(pltpu.make_async_copy(rows, parts, done.at[4]))
    rows[chips:] = early_rows[...]
    for k, term in enumerate(back_terms(0, 2, gathered, weights, blocks)):
        if k < 4:
            scratch[k] = term + early[k][...]
            copies[k].start()
        else:
            rows[:chips, (k - 4) * n : (k - 3) * n, :] = term
    copies[4].start()
    for copy in copies:
        copy.wait()


def collect_kernel(parts, output, input_grad):
    n = output.shape[0]
    output[...] = jnp.sum(parts[:, :n], axis=0)
    input_grad[...] = jnp.sum(parts[:, n:], axis=0)


class Plan:
    def __init__(self, rows, cols):
        self.rows, self.cols = rows, cols

    def flat(self, row, col):
        return row * self.cols + col

    def steps(self, core, col):
        near = 1 if col % 2 == 0 else -1
        far = 2 if (col // 2 + core) % 2 == 0 else -2
        return near, -near, far

    def planes(self):
        return [
            [
                self.flat(2 * chip + core, col)
                for step in (*self.steps(core, col), 0)
                for chip in range((col + step) % 4, self.rows // 2, 4)
            ]
            for core in range(2)
            for col in range(self.cols)
        ]

    def swap(self, k):
        return [
            (self.flat(row, col), self.flat(row, (col + self.steps(row % 2, col)[k]) % self.cols))
            for row in range(self.rows)
            for col in range(self.cols)
        ]

    def quarter(self, core, col):
        return (col // 4 - core) % 4

    def pairs(self, mates):
        groups = []
        for row in range(self.rows):
            for col in range(self.cols):
                at = self.quarter(row % 2, col)
                if mates and at % 2 == 0:
                    groups.append([self.flat(row, col), self.flat(row, (col + 4) % self.cols)])
                if not mates and at < 2:
                    step = 4 if at == 1 else -4
                    groups.append([self.flat(row, col), self.flat(row, (col + step) % self.cols)])
        return groups


def solution(mesh):
    rows, cols = mesh.shape["row"], mesh.shape["col"]
    plan = Plan(rows, cols)
    planes = plan.planes()
    swaps = [plan.swap(k) for k in range(3)]
    core_perm = [(row, row ^ 1) for row in range(rows)]
    across, mates = plan.pairs(False), plan.pairs(True)

    def local(tokens, weight_in, weight_out, cotangent):
        n, d = tokens.shape
        h = weight_in.shape[1]
        chips = rows // 2
        block = (2, 2, chips // 8 * n, 2 * h)
        at = ((lax.axis_index("col") >> 2) - (lax.axis_index("row") & 1)) & 3
        keep = at >> 1

        sent = jnp.broadcast_to(jnp.concatenate([tokens, cotangent], axis=0)[None], (chips, 2 * n, d))
        sent, weight_in, weight_out = lax.optimization_barrier((sent, weight_in, weight_out))
        weight_in_other = lax.ppermute(weight_in, "row", core_perm)
        weight_out_other = lax.ppermute(weight_out, "row", core_perm)
        gathered = lax.all_to_all(sent, BOTH, 0, 0, tiled=True, axis_index_groups=planes)
        weights = (weight_in, weight_in_other, weight_out, weight_out_other)

        col, core = lax.axis_index("col"), lax.axis_index("row") & 1
        near = 1 - 2 * (col & 1)
        far = 2 - 4 * (((col >> 1) + core) & 1)
        keeps = jnp.stack([((((col + step) & (cols - 1)) >> 2) - core & 3) >> 1 for step in (near, -near, far, 0)])
        keeps = keeps.astype(jnp.int32)

        def terms(first, count):
            return kernel_call(
                lambda *refs: sums_kernel(first, *refs),
                [block[1:]] * (2 * count),
                (keeps, gathered, *weights),
                scalars=1,
                far=count > 1,
            )

        away, own = terms(0, 3), terms(3, 1)
        away_given = [lax.ppermute(value, BOTH, perm) for value, perm in zip(away[0::2], swaps)]
        away_kept = [lax.ppermute(value, BOTH, perm) for value, perm in zip(away[1::2], swaps)]
        given = kernel_call(add_kernel, [block[1:]], (own[0], *away_given))[0]

        def swap(value, groups, first):
            got = lax.all_gather(value, BOTH, axis=0, axis_index_groups=groups)
            return jnp.where(first == 0, got[1], got[0])

        got = swap(given, across, keep)
        kept = kernel_call(add_kernel, [block[1:]], (own[1], *away_kept, got))[0]
        kept = kept + swap(kept, mates, at & 1)

        pre, grad = kept[0], kept[1]
        hidden = jnp.stack([gelu_value(pre), grad * gelu_slope(pre)])
        own = lax.all_gather(hidden, BOTH, axis=0, axis_index_groups=across)
        blocks = [lax.ppermute(own, BOTH, perm) for perm in swaps] + [own]

        square = [(d, h)] * 4
        early = kernel_call(early_kernel, [(chips // 2, 2 * n, d)] + square, (gathered, *weights, *blocks[2:]))
        parts, *grads = pl.pallas_call(
            late_kernel,
            out_shape=[pltpu.HBM(shape, jnp.float32) for shape in [(chips, 2 * n, d)] + square],
            in_specs=[VMEM] * 12,
            out_specs=[FAR] * 5,
            scratch_shapes=[
                pltpu.VMEM((chips, 2 * n, d), jnp.float32),
                pltpu.VMEM((4, d, h), jnp.float32),
                pltpu.SemaphoreType.DMA((5,)),
            ],
            compiler_params=pltpu.CompilerParams(vmem_limit_bytes=9 * 2**20),
            cost_estimate=pl.CostEstimate(flops=1000, bytes_accessed=1000, transcendentals=0),
        )(gathered, *weights, *blocks[:2], *early)
        parts = lax.all_to_all(parts, BOTH, 0, 0, tiled=True, axis_index_groups=planes)
        weight_out_grad = grads[2] + lax.ppermute(grads[0], "row", core_perm)
        weight_in_grad = grads[3] + lax.ppermute(grads[1], "row", core_perm)
        output, input_grad = kernel_call(collect_kernel, [(n, d)] * 2, (parts,))
        return (output, input_grad, weight_in_grad, weight_out_grad)

    placed = (P("row", "col"), P("col", "row"), P("row", "col"), P("row", "col"))
    return jax.shard_map(
        local,
        mesh=mesh,
        in_specs=placed,
        out_specs=(P("row", "col"), P("row", "col"), P("col", "row"), P("row", "col")),
        check_vma=False,
    )
```

```python
import math

import jax
import jax.numpy as jnp
from jax import lax
from jax.experimental import pallas as pl
from jax.experimental.pallas import tpu as pltpu
from jax.sharding import PartitionSpec as P

BOTH = ("row", "col")
VMEM = pl.BlockSpec(memory_space=pltpu.VMEM)
SMEM = pl.BlockSpec(memory_space=pltpu.SMEM)
FAR = pl.BlockSpec(memory_space=pltpu.HBM)


def gelu_value(pre):
    return pre * 0.5 * (1.0 + jax.scipy.special.erf(pre / math.sqrt(2.0)))


def gelu_slope(pre):
    cumulative = 0.5 * (1.0 + jax.scipy.special.erf(pre / math.sqrt(2.0)))
    density = jnp.exp(-0.5 * pre * pre) / math.sqrt(2.0 * math.pi)
    return cumulative + pre * density


def split(value):
    high = value.astype(jnp.bfloat16)
    return high, (value - high.astype(jnp.float32)).astype(jnp.bfloat16)


def three(left, right, dims):
    def one(a, b):
        return lax.dot_general(a, b, (dims, ((), ())), preferred_element_type=jnp.float32)

    (lh, ll), (rh, rl) = left, right
    return one(lh, rh) + (one(lh, rl) + one(ll, rh))


PLAIN, RIGHT_T, LEFT_T = ((1,), (0,)), ((1,), (1,)), ((0,), (0,))


def kernel_call(body, out_shapes, args, scalars=0, far=False):
    out = [pltpu.HBM(shape, jnp.float32) if far else jax.ShapeDtypeStruct(shape, jnp.float32) for shape in out_shapes]
    return pl.pallas_call(
        body,
        out_shape=out,
        in_specs=[SMEM] * scalars + [VMEM] * (len(args) - scalars),
        out_specs=[VMEM] * len(out),
        compiler_params=pltpu.CompilerParams(vmem_limit_bytes=9 * 2**20),
        cost_estimate=pl.CostEstimate(flops=1000, bytes_accessed=1000, transcendentals=0),
    )(*args)


def token_rows(gathered, first, last, which):
    n, d = gathered.shape[1] // 2, gathered.shape[2]
    return gathered[first:last, which * n : (which + 1) * n, :].reshape((last - first) * n, d)


def sums_kernel(first, keeps, gathered, w_in, w_in_other, w_out, w_out_other, *outs):
    count = len(outs) // 2
    n, d = gathered.shape[1] // 2, gathered.shape[2]
    half = gathered.shape[0] // 8
    for which, (weights, dims) in enumerate((((w_in, w_in_other), PLAIN), ((w_out, w_out_other), RIGHT_T))):
        rows = []
        for i in range(first, first + count):
            for part in (1 - keeps[i], keeps[i]):
                chips = pl.ds((2 * i + part) * half, half)
                rows.append(gathered[chips, which * n : (which + 1) * n, :].reshape(half * n, d))
        rows = split(jnp.concatenate(rows, axis=0))
        for k in range(2):
            term = three(rows, split(weights[k][...]), dims)
            for i, out in enumerate(outs):
                out[which, :, k * d : (k + 1) * d] = term[i * half * n : (i + 1) * half * n]


def add_kernel(*refs):
    total = refs[0][...]
    for ref in refs[1:-1]:
        total = total + ref[...]
    refs[-1][...] = total


def hidden_rows(blocks, which):
    return jnp.concatenate([block[part, which] for block in blocks for part in range(2)], axis=0)


def back_terms(first, count, gathered, weights, blocks):
    size = gathered.shape[2]
    quarter = gathered.shape[0] // 4
    begin, end = first * quarter, (first + count) * quarter
    act, slope = split(hidden_rows(blocks, 0)), split(hidden_rows(blocks, 1))
    tokens, cotangent = (split(token_rows(gathered, begin, end, which)) for which in range(2))
    for k in range(2):
        at = slice((1 - k) * size, (2 - k) * size)
        yield three([v[:, at] for v in act], cotangent, LEFT_T)
        yield three(tokens, [v[:, at] for v in slope], LEFT_T)
    shape = (count * quarter, gathered.shape[1] // 2, size)
    w_in, w_in_other, w_out, w_out_other = weights
    for hidden, pair, dims in ((act, (w_out, w_out_other), PLAIN), (slope, (w_in, w_in_other), RIGHT_T)):
        term = [
            three([v[:, k * size : (k + 1) * size] for v in hidden], split(pair[k][...]), dims) for k in range(2)
        ]
        yield (term[0] + term[1]).reshape(shape)


def early_kernel(gathered, *refs):
    weights, blocks, (rows, *grads) = refs[:4], refs[4:6], refs[6:]
    n = rows.shape[1] // 2
    for k, term in enumerate(back_terms(2, 2, gathered, weights, blocks)):
        if k < 4:
            grads[k][...] = term
        else:
            rows[:, (k - 4) * n : (k - 3) * n, :] = term


def late_kernel(gathered, *refs):
    weights, blocks, (early_rows, *early), refs = refs[:4], refs[4:6], refs[6:11], refs[11:]
    parts, grads, rows, scratch, done = refs[0], refs[1:5], refs[5], refs[6], refs[7]
    n = rows.shape[1] // 2
    chips = rows.shape[0] // 2
    copies = [pltpu.make_async_copy(scratch.at[k], grads[k], done.at[k]) for k in range(4)]
    copies.append(pltpu.make_async_copy(rows, parts, done.at[4]))
    rows[chips:] = early_rows[...]
    for k, term in enumerate(back_terms(0, 2, gathered, weights, blocks)):
        if k < 4:
            scratch[k] = term + early[k][...]
            copies[k].start()
        else:
            rows[:chips, (k - 4) * n : (k - 3) * n, :] = term
    copies[4].start()
    for copy in copies:
        copy.wait()


def collect_kernel(parts, output, input_grad):
    n = output.shape[0]
    output[...] = jnp.sum(parts[:, :n], axis=0)
    input_grad[...] = jnp.sum(parts[:, n:], axis=0)


class Plan:
    def __init__(self, rows, cols):
        self.rows, self.cols = rows, cols

    def flat(self, row, col):
        return row * self.cols + col

    def steps(self, core, col):
        near = 1 if col % 2 == 0 else -1
        far = 2 if (col // 2 + core) % 2 == 0 else -2
        return near, -near, far

    def planes(self):
        return [
            [
                self.flat(2 * chip + core, col)
                for step in (*self.steps(core, col), 0)
                for chip in range((col + step) % 4, self.rows // 2, 4)
            ]
            for core in range(2)
            for col in range(self.cols)
        ]

    def swap(self, k):
        return [
            (self.flat(row, col), self.flat(row, (col + self.steps(row % 2, col)[k]) % self.cols))
            for row in range(self.rows)
            for col in range(self.cols)
        ]

    def quarter(self, core, col):
        return (col // 4 - core) % 4

    def pairs(self, mates):
        groups = []
        for row in range(self.rows):
            for col in range(self.cols):
                at = self.quarter(row % 2, col)
                if mates and at % 2 == 0:
                    groups.append([self.flat(row, col), self.flat(row, (col + 4) % self.cols)])
                if not mates and at < 2:
                    step = 4 if at == 1 else -4
                    groups.append([self.flat(row, col), self.flat(row, (col + step) % self.cols)])
        return groups


def solution(mesh):
    rows, cols = mesh.shape["row"], mesh.shape["col"]
    plan = Plan(rows, cols)
    planes = plan.planes()
    swaps = [plan.swap(k) for k in range(3)]
    core_perm = [(row, row ^ 1) for row in range(rows)]
    across, mates = plan.pairs(False), plan.pairs(True)

    def local(tokens, weight_in, weight_out, cotangent):
        n, d = tokens.shape
        h = weight_in.shape[1]
        chips = rows // 2
        block = (2, 2, chips // 8 * n, 2 * h)
        at = ((lax.axis_index("col") >> 2) - (lax.axis_index("row") & 1)) & 3
        keep = at >> 1

        sent = jnp.broadcast_to(jnp.concatenate([tokens, cotangent], axis=0)[None], (chips, 2 * n, d))
        sent, weight_in, weight_out = lax.optimization_barrier((sent, weight_in, weight_out))
        weight_in_other = lax.ppermute(weight_in, "row", core_perm)
        weight_out_other = lax.ppermute(weight_out, "row", core_perm)
        gathered = lax.all_to_all(sent, BOTH, 0, 0, tiled=True, axis_index_groups=planes)
        weights = (weight_in, weight_in_other, weight_out, weight_out_other)

        col, core = lax.axis_index("col"), lax.axis_index("row") & 1
        near = 1 - 2 * (col & 1)
        far = 2 - 4 * (((col >> 1) + core) & 1)
        keeps = jnp.stack([((((col + step) & (cols - 1)) >> 2) - core & 3) >> 1 for step in (near, -near, far, 0)])
        keeps = keeps.astype(jnp.int32)

        def terms(first, count):
            return kernel_call(
                lambda *refs: sums_kernel(first, *refs),
                [block[1:]] * (2 * count),
                (keeps, gathered, *weights),
                scalars=1,
                far=count > 1,
            )

        every = terms(0, 4)
        away, own = every[:6], every[6:]
        away_given = [lax.ppermute(value, BOTH, perm) for value, perm in zip(away[0::2], swaps)]
        away_kept = [lax.ppermute(value, BOTH, perm) for value, perm in zip(away[1::2], swaps)]
        given = kernel_call(add_kernel, [block[1:]], (own[0], *away_given))[0]

        def swap(value, groups, first):
            got = lax.all_gather(value, BOTH, axis=0, axis_index_groups=groups)
            return jnp.where(first == 0, got[1], got[0])

        got = swap(given, across, keep)
        kept = kernel_call(add_kernel, [block[1:]], (own[1], *away_kept, got))[0]
        kept = kept + swap(kept, mates, at & 1)

        pre, grad = kept[0], kept[1]
        hidden = jnp.stack([gelu_value(pre), grad * gelu_slope(pre)])
        own = lax.all_gather(hidden, BOTH, axis=0, axis_index_groups=across)
        blocks = [lax.ppermute(own, BOTH, perm) for perm in swaps] + [own]

        square = [(d, h)] * 4
        early = kernel_call(early_kernel, [(chips // 2, 2 * n, d)] + square, (gathered, *weights, *blocks[2:]))
        parts, *grads = pl.pallas_call(
            late_kernel,
            out_shape=[pltpu.HBM(shape, jnp.float32) for shape in [(chips, 2 * n, d)] + square],
            in_specs=[VMEM] * 12,
            out_specs=[FAR] * 5,
            scratch_shapes=[
                pltpu.VMEM((chips, 2 * n, d), jnp.float32),
                pltpu.VMEM((4, d, h), jnp.float32),
                pltpu.SemaphoreType.DMA((5,)),
            ],
            compiler_params=pltpu.CompilerParams(vmem_limit_bytes=9 * 2**20),
            cost_estimate=pl.CostEstimate(flops=1000, bytes_accessed=1000, transcendentals=0),
        )(gathered, *weights, *blocks[:2], *early)
        parts = lax.all_to_all(parts, BOTH, 0, 0, tiled=True, axis_index_groups=planes)
        weight_out_grad = grads[2] + lax.ppermute(grads[0], "row", core_perm)
        weight_in_grad = grads[3] + lax.ppermute(grads[1], "row", core_perm)
        output, input_grad = kernel_call(collect_kernel, [(n, d)] * 2, (parts,))
        return (output, input_grad, weight_in_grad, weight_out_grad)

    placed = (P("row", "col"), P("col", "row"), P("row", "col"), P("row", "col"))
    return jax.shard_map(
        local,
        mesh=mesh,
        in_specs=placed,
        out_specs=(P("row", "col"), P("row", "col"), P("col", "row"), P("row", "col")),
        check_vma=False,
    )
```
